256 devices in a mesh: band: 8 (over z_hi, core), domain: 32 (over z_lo, x, y).
Axes of the slice: x: 4, y: 4, z: 8 (z_hi: 4, z_lo: 2; z = z_hi * 2 + z_lo), core: 2. Of those that a mesh axis runs over, the one named last changes fastest.
Arguments:
- states: float32 [32, 192, 16, 128], P('band', 'domain'), may hold values from -6 to 6
- potential: float32 [192, 16, 128], P('domain'), may hold values from -10 to 2
- slab: bfloat16 [256, 192, 16, 128], P('band', 'domain'), may hold values from -6 to 6
Outputs:
- gram: float32 [32, 256], P('domain', 'band')
- projected: float32 [32, 256], P('domain', 'band')
The draws below stay inside these ranges and needn't reach their ends.
All inputs are finite; a program needn't handle non-finite values.
Results may differ from the reference program's by a relative error of at most 0.0045.
Values may be sent and summed in bfloat16 or wider, within the bound.
No kernel may reach another device: no remote copies, remote signals or barrier semaphores. Data moves between devices by JAX's collectives and lax.ppermute only.
A program may use at most 192 MiB of HBM per device.

```python
import jax
import jax.numpy as jnp

STATES = 32
SLAB = 256
CY = 16
CZ = 128
NX = 192


def levels(stream_key, shape, cuts, least, high):
    def one(position, blocks):
        draws = jax.random.uniform(jax.random.fold_in(jax.random.fold_in(stream_key, 6), position), (blocks,), jnp.float32, least / len(cuts), high / len(cuts))
        return jnp.repeat(jnp.exp(draws), shape[position] // blocks).reshape((-1,) + (1,) * (len(shape) - position - 1))

    level = one(*cuts[0])
    for cut in cuts[1:]:
        level = level * one(*cut)
    return level


def scatter_about(stream_key, dims, scale, bound, shards=(), kind=jnp.bfloat16):
    gain = levels(stream_key, dims, shards, -0.22, 0.18) if shards else 1.0
    entries = jax.random.normal(stream_key, dims, jnp.float32) * scale * gain
    return jnp.minimum(jnp.maximum(entries, -bound), bound).astype(kind)


def setup_inputs(seed: int = 0) -> dict:
    key_of = jax.random.split(jax.random.key(seed), 4)
    states = scatter_about(key_of[0], (STATES, NX, CY, CZ), 1.0, 6.0, ((0, 8), (1, 32)), jnp.float32)
    potential = jnp.clip(-10.0 + 12.0 * jax.random.uniform(key_of[1], (NX, CY, CZ), jnp.float32) ** levels(key_of[1], (NX, CY, CZ), ((0, 32),), -0.2, 0.2), -10.0, 2.0)
    slab = scatter_about(key_of[2], (SLAB, NX, CY, CZ), 1.0, 6.0, ((0, 8), (1, 32)))
    return {"states": states, "potential": potential, "slab": slab}


COEFS = (-5369.0 / 1800.0, 12.0 / 7.0, -15.0 / 56.0, 10.0 / 189.0, -1.0 / 112.0, 2.0 / 1925.0, -1.0 / 16632.0)
SPACING = 0.5
CENTER = 27.5
HALF = 22.5

def hamiltonian(field, potential):
    total = 3.0 * COEFS[0] * field
    for reach in range(1, 7):
        for axis_pos in (-3, -2, -1):
            total = total + COEFS[reach] * (jnp.roll(field, reach, axis_pos) + jnp.roll(field, -reach, axis_pos))
    return -0.5 / SPACING ** 2 * total + potential * field

def reference(states, potential, slab):
    first = (hamiltonian(states, potential) - CENTER * states) / HALF
    second = 2.0 * (hamiltonian(first, potential) - CENTER * first) / HALF - states
    rounded = second.astype(jnp.bfloat16)
    applied = (hamiltonian(rounded.astype(jnp.float32), potential) / HALF).astype(jnp.bfloat16)
    slab_flat = slab.reshape(slab.shape[0], -1)
    scale = 1.0 / jnp.sqrt(jnp.float32(slab_flat.shape[1]))
    gram = jnp.dot(rounded.reshape(rounded.shape[0], -1), slab_flat.T, preferred_element_type=jnp.float32) * scale
    projected = jnp.dot(applied.reshape(applied.shape[0], -1), slab_flat.T, preferred_element_type=jnp.float32) * scale
    return (gram, projected)
```

```python
import functools

import jax
import jax.numpy as jnp
from jax import lax
from jax.experimental import pallas as pl
from jax.experimental.pallas import tpu as pltpu
from jax.sharding import Mesh, PartitionSpec as P

COEFS = (
    -5369.0 / 1800.0,
    12.0 / 7.0,
    -15.0 / 56.0,
    10.0 / 189.0,
    -1.0 / 112.0,
    2.0 / 1925.0,
    -1.0 / 16632.0,
)
SPACING = 0.5
CENTER = 27.5
HALF = 22.5
KIN = -0.5 / SPACING**2
OFF = tuple(KIN * c / HALF for c in COEFS)
DIAG = 3.0 * KIN * COEFS[0] / HALF
BAND = ("z_hi", "core")
DOMAIN = ("z_lo", "x", "y")
CELLS = 393216
W = 6


def stencil(ref, at, scaled):
    v = ref[at]
    total = (DIAG + scaled) * v
    for k in range(1, W + 1):
        along = ref[at + k] + ref[at - k]
        along = along + pltpu.roll(v, k, 0) + pltpu.roll(v, 16 - k, 0)
        along = along + pltpu.roll(v, k, 1) + pltpu.roll(v, 128 - k, 1)
        total = total + OFF[k] * along
    return total


def filter_kernel(m2, m1, s, p1, p2, pot_m, pot, pot_p, out, field, first, scaled):
    planes = s.shape[1]
    scaled[0:planes] = pot_m[...] * (1.0 / HALF)
    scaled[planes : 2 * planes] = pot[...] * (1.0 / HALF)
    scaled[2 * planes : 3 * planes] = pot_p[...] * (1.0 / HALF)

    def one(i, _):
        for j, ref in enumerate((m2, m1, s, p1, p2)):
            field[j * planes : (j + 1) * planes] = ref[i].astype(jnp.float32)

        def inner(x, _):
            v = field[x + W]
            first[x] = stencil(field, x + W, scaled[x]) - (CENTER / HALF) * v
            return 0

        lax.fori_loop(0, 3 * planes, inner, 0, unroll=2)

        def outer(x, _):
            v = first[x + W]
            t = stencil(first, x + W, scaled[x + W]) - (CENTER / HALF) * v
            out[i, x] = (2.0 * t - field[x + 2 * W]).astype(jnp.bfloat16)
            return 0

        lax.fori_loop(0, planes, outer, 0, unroll=2)
        return 0

    lax.fori_loop(0, s.shape[0], one, 0)


def apply_kernel(m1, r, p1, pot, out, field):
    planes = r.shape[1]

    def one(i, _):
        for j, ref in enumerate((m1, r, p1)):
            field[j * planes : (j + 1) * planes] = ref[i].astype(jnp.float32)

        def inner(x, _):
            out[i, x] = stencil(field, x + W, pot[x] * (1.0 / HALF)).astype(jnp.bfloat16)
            return 0

        lax.fori_loop(0, planes, inner, 0, unroll=2)
        return 0

    lax.fori_loop(0, r.shape[0], one, 0)


def shifted(array, by):
    n = 32
    return lax.ppermute(array, DOMAIN, [(i, (i + by) % n) for i in range(n)])


def body(states, potential, slab):
    count, planes = states.shape[:2]
    low = states.astype(jnp.bfloat16)
    m1, p1 = shifted(low, 1), shifted(low, -1)
    m2, p2 = shifted(low, 2), shifted(low, -2)
    pot_m, pot_p = shifted(potential, 1), shifted(potential, -1)
    f32 = jnp.float32
    block = jax.ShapeDtypeStruct(states.shape, jnp.bfloat16)
    vm = pl.BlockSpec(memory_space=pltpu.VMEM)
    grid = states.shape[2:]
    rounded = pl.pallas_call(
        filter_kernel,
        out_shape=block,
        in_specs=[vm] * 8,
        out_specs=vm,
        scratch_shapes=[
            pltpu.VMEM((5 * planes, *grid), f32),
            pltpu.VMEM((3 * planes, *grid), f32),
            pltpu.VMEM((3 * planes, *grid), f32),
        ],
        cost_estimate=pl.CostEstimate(flops=10_000_000, bytes_accessed=700_000, transcendentals=0),
    )(m2, m1, states, p1, p2, pot_m, potential, pot_p)
    rm, rp = shifted(rounded, 1), shifted(rounded, -1)
    gathered = lax.all_gather(rounded, BAND, axis=0, tiled=True)
    applied = pl.pallas_call(
        apply_kernel,
        out_shape=block,
        in_specs=[vm] * 4,
        out_specs=vm,
        scratch_shapes=[pltpu.VMEM((3 * planes, *grid), f32)],
        cost_estimate=pl.CostEstimate(flops=3_000_000, bytes_accessed=400_000, transcendentals=0),
    )(rm, rounded, rp, potential)
    gathered_applied = lax.all_gather(applied, BAND, axis=0, tiled=True)

    slab_flat = slab.reshape(slab.shape[0], -1)

    def products(x):
        flat = x.reshape(x.shape[0], -1)
        return lax.dot_general(flat, slab_flat, (((1,), (1,)), ((), ())), preferred_element_type=f32)

    term = jnp.concatenate([products(gathered), products(gathered_applied)], axis=1)
    parts = lax.all_to_all(term, DOMAIN, 0, 0, tiled=True)
    scale = 1.0 / jnp.sqrt(jnp.float32(CELLS))
    share = jnp.sum(parts, axis=0, keepdims=True) * scale
    n = slab.shape[0]
    return share[:, :n], share[:, n:]


def solution(mesh):
    fine = Mesh(mesh.devices.reshape(4, 2, 2, 4, 4), ("z_hi", "core", "z_lo", "x", "y"))
    placed = (P(BAND, DOMAIN, None, None), P(DOMAIN, None, None), P(BAND, DOMAIN, None, None))
    return jax.shard_map(
        body,
        mesh=fine,
        in_specs=placed,
        out_specs=(P(DOMAIN, BAND), P(DOMAIN, BAND)),
        check_vma=False,
    )
```

```python
import jax
import jax.numpy as jnp
import ml_dtypes
import numpy as np
from jax import lax
from jax.experimental import pallas as pl
from jax.experimental.pallas import tpu as pltpu
from jax.sharding import Mesh, PartitionSpec as P

COEFS = (
    -5369.0 / 1800.0,
    12.0 / 7.0,
    -15.0 / 56.0,
    10.0 / 189.0,
    -1.0 / 112.0,
    2.0 / 1925.0,
    -1.0 / 16632.0,
)
SPACING = 0.5
CENTER = 27.5
HALF = 22.5
KIN = -0.5 / SPACING**2
OFF = tuple(KIN * c / HALF for c in COEFS)
DIAG = 3.0 * KIN * COEFS[0] / HALF
SHIFT = CENTER / HALF
BAND = ("z_hi", "core")
DOMAIN = ("z_lo", "x", "y")
CELLS = 393216
W = 6
CY, CZ, PLANES = 16, 128, 6
ROWS = PLANES * CY
BF16, F32 = jnp.bfloat16, jnp.float32


def circulant(n):
    m = np.zeros((n, n), np.float64)
    for i in range(n):
        for k in range(1, W + 1):
            m[i, (i + k) % n] += OFF[k]
            m[i, (i - k) % n] += OFF[k]
    return m


def halves(m):
    high = m.astype(ml_dtypes.bfloat16)
    low = (m - high.astype(np.float64)).astype(ml_dtypes.bfloat16)
    return high, low


Z_HIGH, Z_LOW = halves(circulant(CZ))
Y_HIGH, Y_LOW = halves(np.kron(np.eye(PLANES), circulant(CY)))
Z2 = np.concatenate([Z_HIGH, Z_LOW], 0)
Y2 = np.concatenate([Y_HIGH, Y_LOW], 1)
Z3 = np.block([[Z_HIGH, Z_LOW], [Z_HIGH, np.zeros_like(Z_LOW)]])
Y3 = np.concatenate([Y_HIGH, Y_HIGH, Y_LOW], 1)


def dot(a, b):
    return jnp.dot(a, b, preferred_element_type=F32)


def along_x(planes, n):
    out = []
    for x in range(W, W + n):
        total = OFF[1] * (planes[x + 1] + planes[x - 1])
        for k in range(2, W + 1):
            total = total + OFF[k] * (planes[x + k] + planes[x - k])
        out.append(total)
    return out


def along_yz(planes, z3, y3):
    n = len(planes)
    field = jnp.concatenate([p[None] for p in planes], 0).reshape(n * CY, CZ)
    high = field.astype(BF16)
    low = (field - high.astype(F32)).astype(BF16)
    z = dot(jnp.concatenate([high, low], 1), z3)
    z = z[:, :CZ] + z[:, CZ:]
    out = []
    for g in range(0, n * CY, ROWS):
        h, l = high[g : g + ROWS], low[g : g + ROWS]
        y = dot(y3, jnp.concatenate([h, l, h], 0)) + z[g : g + ROWS]
        out += [y[i * CY : (i + 1) * CY] for i in range(PLANES)]
    return out


def filter_kernel(m2, m1, s, p1, p2, pot, z3_ref, y3_ref, out):
    count = s.shape[0]
    z3, y3 = z3_ref[...], y3_ref[...]

    def sent(ref):
        return [(ref[count, x].astype(F32) + ref[count + 1, x].astype(F32)) for x in range(PLANES)]

    raw = sent(m1) + [pot[x] for x in range(PLANES)] + sent(p1)
    diag = [(DIAG - SHIFT) + v * (1.0 / HALF) for v in raw]
    for i in range(count):
        field = []
        for ref in (m2, m1, s, p1, p2):
            field += [ref[i, x].astype(F32) for x in range(PLANES)]
        inner = field[W:-W]
        first = [
            a + b + d * v
            for a, b, d, v in zip(along_x(field, 3 * PLANES), along_yz(inner, z3, y3), diag, inner)
        ]
        own = first[W:-W]
        turned = [
            a + b + d * v
            for a, b, d, v in zip(along_x(first, PLANES), along_yz(own, z3, y3), diag[W:-W], own)
        ]
        for x in range(PLANES):
            out[i, x] = (2.0 * turned[x] - field[2 * W + x]).astype(BF16)


def slab_inner_kernel(slab, pot, z2_ref, y2_ref, out):
    count = slab.shape[0]
    z2, y2 = z2_ref[...], y2_ref[...]
    diag = (DIAG + pot[...] * (1.0 / HALF)).reshape(ROWS, CZ)
    for i in range(0, count, 2):
        pair = [slab[i + j].reshape(ROWS, CZ) for j in range(2)]
        wide = jnp.concatenate(pair, 1)
        y = dot(y2, jnp.concatenate([wide, wide], 0))
        for j in range(2):
            z = dot(jnp.concatenate([pair[j], pair[j]], 1), z2)
            total = y[:, j * CZ : (j + 1) * CZ] + z + diag * pair[j].astype(F32)
            out[i + j] = total.reshape(PLANES, CY, CZ)


def slab_outer_kernel(before, slab, after, inner, out):
    def one(i, _):
        planes = []
        for ref in (before, slab, after):
            planes += [ref[i, x].astype(F32) for x in range(PLANES)]
        for x, along in enumerate(along_x(planes, PLANES)):
            out[i, x] = (along + inner[i, x]).astype(BF16)
        return 0

    lax.fori_loop(0, slab.shape[0], one, 0)


def shifted(array, by):
    n = 32
    return lax.ppermute(array, DOMAIN, [(i, (i + by) % n) for i in range(n)])


def vmem(n=1):
    return [pl.BlockSpec(memory_space=pltpu.VMEM)] * n


def filter_own(m2, m1, s, p1, p2, pot):
    return pl.pallas_call(
        filter_kernel,
        out_shape=jax.ShapeDtypeStruct(s.shape, BF16),
        in_specs=vmem(8),
        out_specs=vmem()[0],
        compiler_params=pltpu.CompilerParams(vmem_limit_bytes=16 << 20),
        cost_estimate=pl.CostEstimate(flops=200_000_000, bytes_accessed=800_000, transcendentals=0),
        name="filter_own",
    )(m2, m1, s, p1, p2, pot, jnp.asarray(Z3), jnp.asarray(Y3))


GROUP = 8


def by_group(count):
    return pl.BlockSpec((GROUP, PLANES, CY, CZ), lambda i: (i, 0, 0, 0))


def whole(shape):
    return pl.BlockSpec(shape, lambda i: (0,) * len(shape))


def slab_inner(slab, pot):
    n = slab.shape[0]
    return pl.pallas_call(
        slab_inner_kernel,
        grid=(n // GROUP,),
        out_shape=jax.ShapeDtypeStruct(slab.shape, F32),
        in_specs=[by_group(n), whole(pot.shape), whole(Z2.shape), whole(Y2.shape)],
        out_specs=by_group(n),
        compiler_params=pltpu.CompilerParams(vmem_limit_bytes=16 << 20),
        cost_estimate=pl.CostEstimate(flops=400_000_000, bytes_accessed=2_400_000, transcendentals=0),
        name="slab_inner",
    )(slab, pot, jnp.asarray(Z2), jnp.asarray(Y2))


def slab_outer(before, slab, after, inner):
    n = slab.shape[0]
    return pl.pallas_call(
        slab_outer_kernel,
        grid=(n // GROUP,),
        out_shape=jax.ShapeDtypeStruct(slab.shape, BF16),
        in_specs=[by_group(n)] * 4,
        out_specs=by_group(n),
        compiler_params=pltpu.CompilerParams(vmem_limit_bytes=16 << 20),
        cost_estimate=pl.CostEstimate(flops=10_000_000, bytes_accessed=4_700_000, transcendentals=0),
        name="slab_outer",
    )(before, slab, after, inner)


def body(states, potential, slab):
    low = states.astype(BF16)
    pot_high = potential.astype(BF16)
    pot_low = (potential - pot_high.astype(F32)).astype(BF16)
    near = jnp.concatenate([low, pot_high[None], pot_low[None]], axis=0)
    m1, p1 = shifted(near, 1), shifted(near, -1)
    m2, p2 = shifted(low, 2), shifted(low, -2)
    inner = slab_inner(slab, potential)
    late_slab, inner = lax.optimization_barrier((slab, inner))
    before, after = shifted(late_slab, 1), shifted(late_slab, -1)
    rounded = filter_own(m2, m1, states, p1, p2, potential)
    gathered = lax.all_gather(rounded, BAND, axis=0, tiled=True)
    turned = slab_outer(before, slab, after, inner)

    flat = gathered.reshape(gathered.shape[0], -1)

    def products(x):
        return lax.dot_general(
            flat, x.reshape(x.shape[0], -1), (((1,), (1,)), ((), ())), preferred_element_type=F32
        )

    term = jnp.concatenate([products(slab), products(turned)], axis=1)
    parts = lax.all_to_all(term, DOMAIN, 0, 0, tiled=True)
    scale = 1.0 / jnp.sqrt(jnp.float32(CELLS))
    share = jnp.sum(parts, axis=0, keepdims=True) * scale
    n = slab.shape[0]
    return share[:, :n], share[:, n:]


def solution(mesh):
    fine = Mesh(mesh.devices.reshape(4, 2, 2, 4, 4), ("z_hi", "core", "z_lo", "x", "y"))
    placed = (P(BAND, DOMAIN, None, None), P(DOMAIN, None, None), P(BAND, DOMAIN, None, None))
    return jax.shard_map(
        body,
        mesh=fine,
        in_specs=placed,
        out_specs=(P(DOMAIN, BAND), P(DOMAIN, BAND)),
        check_vma=False,
    )
```

```python
import jax
import jax.numpy as jnp
import ml_dtypes
import numpy as np
from jax import lax
from jax.experimental import pallas as pl
from jax.experimental.pallas import tpu as pltpu
from jax.sharding import Mesh, PartitionSpec as P

COEFS = (
    -5369.0 / 1800.0,
    12.0 / 7.0,
    -15.0 / 56.0,
    10.0 / 189.0,
    -1.0 / 112.0,
    2.0 / 1925.0,
    -1.0 / 16632.0,
)
SPACING = 0.5
CENTER = 27.5
HALF = 22.5
KIN = -0.5 / SPACING**2
OFF = tuple(KIN * c / HALF for c in COEFS)
DIAG = 3.0 * KIN * COEFS[0] / HALF
SHIFT = CENTER / HALF
BAND = ("z_hi", "core")
DOMAIN = ("z_lo", "x", "y")
CELLS = 393216
W = 6
CY, CZ, PLANES = 16, 128, 6
ROWS = PLANES * CY
BF16, F32 = jnp.bfloat16, jnp.float32


def circulant(n):
    m = np.zeros((n, n), np.float64)
    for i in range(n):
        for k in range(1, W + 1):
            m[i, (i + k) % n] += OFF[k]
            m[i, (i - k) % n] += OFF[k]
    return m


def plane_weights():
    m = np.zeros((PLANES, 3 * PLANES), np.float64)
    for i in range(PLANES):
        for j in range(3 * PLANES):
            k = abs(i + PLANES - j)
            if 1 <= k <= W:
                m[i, j] = OFF[k]
    m = np.kron(m, np.eye(CY))
    m[:, ROWS : 2 * ROWS] += np.kron(np.eye(PLANES), circulant(CY))
    return m


def halves(m):
    high = m.astype(ml_dtypes.bfloat16)
    low = (m - high.astype(np.float64)).astype(ml_dtypes.bfloat16)
    return high, low


Z_HIGH, Z_LOW = halves(circulant(CZ))
Y_HIGH, Y_LOW = halves(np.kron(np.eye(PLANES), circulant(CY)))
Z3 = np.block([[Z_HIGH, Z_LOW], [Z_HIGH, np.zeros_like(Z_LOW)]])
Y3 = np.concatenate([Y_HIGH, Y_HIGH, Y_LOW], 1)
Z2 = np.concatenate([Z_HIGH, Z_LOW], 0)
XY2 = np.concatenate(halves(plane_weights()), 1)


def dot(a, b):
    return jnp.dot(a, b, preferred_element_type=F32)


def along_x(planes, n):
    out = []
    for x in range(W, W + n):
        total = OFF[1] * (planes[x + 1] + planes[x - 1])
        for k in range(2, W + 1):
            total = total + OFF[k] * (planes[x + k] + planes[x - k])
        out.append(total)
    return out


def along_yz(planes, z3, y3):
    n = len(planes)
    field = jnp.concatenate([p[None] for p in planes], 0).reshape(n * CY, CZ)
    high = field.astype(BF16)
    low = (field - high.astype(F32)).astype(BF16)
    z = dot(jnp.concatenate([high, low], 1), z3)
    z = z[:, :CZ] + z[:, CZ:]
    out = []
    for g in range(0, n * CY, ROWS):
        h, l = high[g : g + ROWS], low[g : g + ROWS]
        y = dot(y3, jnp.concatenate([h, l, h], 0)) + z[g : g + ROWS]
        out += [y[i * CY : (i + 1) * CY] for i in range(PLANES)]
    return out


def filter_kernel(
    even, odd, even2, odd2, even3, odd3, s, pot, z3_ref, y3_ref, z2_ref, xy2_ref, out
):
    count = s.shape[0]
    place = lax.axis_index("y")
    first_of_pair = place % 2 == 0
    first_of_two = place < 2
    z3, y3, z2, xy2 = z3_ref[...], y3_ref[...], z2_ref[...], xy2_ref[...]

    def sides(i, one, other, flag):
        before, after = [], []
        for x in range(PLANES):
            a, b = one[i, x].astype(F32), other[i, x].astype(F32)
            before.append(jnp.where(flag, b, a))
            after.append(jnp.where(flag, a, b))
        return before, after

    def sums(one, other, flag):
        high, low = sides(count, one, other, flag), sides(count + 1, one, other, flag)
        return [[h + l for h, l in zip(*pair)] for pair in zip(high, low)]

    b1, a1 = sums(even, odd, first_of_pair)
    b2, a2 = sums(even2, odd2, first_of_two)
    raw = b2 + b1 + [pot[x] for x in range(PLANES)] + a1 + a2
    diag = [(DIAG - SHIFT) + v * (1.0 / HALF) for v in raw]

    def turn(planes, weights):
        inner = planes[W:-W]
        x = along_x(planes, len(inner))
        yz = along_yz(inner, z3, y3)
        return [a + b + d * v for a, b, d, v in zip(x, yz, weights, inner)]

    for i in range(count):
        b1, a1 = sides(i, even, odd, first_of_pair)
        b2, a2 = sides(i, even2, odd2, first_of_two)
        b3, a3 = sides(i, even3, odd3, first_of_pair)
        field = b3 + b2 + b1 + [s[i, x] for x in range(PLANES)] + a1 + a2 + a3
        first = turn(field, diag)
        second = turn(first, diag[W:-W])
        rounded = [
            (2.0 * t - v).astype(BF16) for t, v in zip(second, field[2 * W : -2 * W])
        ]
        blocks = [jnp.concatenate(rounded[k * W : (k + 1) * W], 0) for k in range(3)]
        own = blocks[1]
        xy = dot(xy2, jnp.concatenate(blocks + blocks, 0))
        z = dot(jnp.concatenate([own, own], 1), z2)
        for x in range(PLANES):
            rows = slice(x * CY, (x + 1) * CY)
            total = xy[rows] + z[rows] + (diag[2 * W + x] + SHIFT) * rounded[W + x].astype(F32)
            out[i, x] = rounded[W + x]
            out[count + i, x] = total.astype(BF16)


def exchange(array, axes, size, partner):
    return lax.ppermute(array, axes, [(i, partner(i) % size) for i in range(size)])


def even_pairs(array):
    return exchange(array, DOMAIN, 32, lambda d: d ^ 1)


def odd_pairs(array):
    return exchange(array, DOMAIN, 32, lambda d: d + 1 if d % 2 else d - 1)


def even_twos(array):
    return exchange(array, DOMAIN, 32, lambda d: d ^ 2)


def odd_twos(array):
    return exchange(array, DOMAIN, 32, lambda d: d + 2 if d % 4 >= 2 else d - 2)


def even_threes(array):
    return exchange(array, DOMAIN, 32, lambda d: d - 3 if d % 2 else d + 3)


def odd_threes(array):
    return exchange(array, DOMAIN, 32, lambda d: d + 3 if d % 2 else d - 3)


def vmem(n=1):
    return [pl.BlockSpec(memory_space=pltpu.VMEM)] * n


def filter_own(pairs, twos, threes, s, pot):
    constants = [jnp.asarray(m) for m in (Z3, Y3, Z2, XY2)]
    return pl.pallas_call(
        filter_kernel,
        out_shape=jax.ShapeDtypeStruct((2 * s.shape[0], *s.shape[1:]), BF16),
        in_specs=vmem(12),
        out_specs=vmem()[0],
        compiler_params=pltpu.CompilerParams(vmem_limit_bytes=16 << 20),
        cost_estimate=pl.CostEstimate(flops=400_000_000, bytes_accessed=1_500_000, transcendentals=0),
        name="filter_own",
    )(*pairs, *twos, *threes, s, pot, *constants)


def body(states, potential, slab):
    count = states.shape[0]
    low = states.astype(BF16)
    pot_high = potential.astype(BF16)
    pot_low = (potential - pot_high.astype(F32)).astype(BF16)
    near = jnp.concatenate([low, pot_high[None], pot_low[None]], axis=0)
    pairs = even_pairs(near), odd_pairs(near)
    twos = even_twos(near), odd_twos(near)
    threes = even_threes(low), odd_threes(low)
    both = filter_own(pairs, twos, threes, states, potential)
    mine = lax.all_gather(both, "z_hi", axis=0, tiled=True)
    theirs = exchange(mine, "core", 2, lambda i: i ^ 1)

    n = slab.shape[0]
    slab_flat = slab.reshape(n, -1)

    def products(block):
        flat = block.reshape(block.shape[0], -1)
        out = lax.dot_general(
            flat, slab_flat, (((1,), (1,)), ((), ())), preferred_element_type=F32
        )
        return jnp.swapaxes(out.reshape(4, 2, count, n), 1, 2)

    pair = jnp.stack([products(mine), products(theirs)], axis=1)
    pair = jnp.where(lax.axis_index("core") == 1, jnp.flip(pair, 1), pair)
    term = pair.reshape(32, 2 * n)
    parts = lax.all_to_all(term, DOMAIN, 0, 0, tiled=True)
    scale = 1.0 / jnp.sqrt(jnp.float32(CELLS))
    share = jnp.sum(parts, axis=0, keepdims=True) * scale
    return share[:, :n], share[:, n:]


def solution(mesh):
    fine = Mesh(mesh.devices.reshape(4, 2, 2, 4, 4), ("z_hi", "core", "z_lo", "x", "y"))
    placed = (P(BAND, DOMAIN, None, None), P(DOMAIN, None, None), P(BAND, DOMAIN, None, None))
    return jax.shard_map(
        body,
        mesh=fine,
        in_specs=placed,
        out_specs=(P(DOMAIN, BAND), P(DOMAIN, BAND)),
        check_vma=False,
    )
```

```python
import jax
import jax.numpy as jnp
import ml_dtypes
import numpy as np
from jax import lax
from jax.experimental import pallas as pl
from jax.experimental.pallas import tpu as pltpu
from jax.sharding import Mesh, PartitionSpec as P

COEFS = (
    -5369.0 / 1800.0,
    12.0 / 7.0,
    -15.0 / 56.0,
    10.0 / 189.0,
    -1.0 / 112.0,
    2.0 / 1925.0,
    -1.0 / 16632.0,
)
SPACING = 0.5
CENTER = 27.5
HALF = 22.5
KIN = -0.5 / SPACING**2
OFF = tuple(KIN * c / HALF for c in COEFS)
DIAG = 3.0 * KIN * COEFS[0] / HALF
SHIFT = CENTER / HALF
BAND = ("z_hi", "core")
DOMAIN = ("z_lo", "x", "y")
CELLS = 393216
W = 6
CY, CZ, PLANES = 16, 128, 6
ROWS = PLANES * CY
BF16, F32 = jnp.bfloat16, jnp.float32


def circulant(n):
    m = np.zeros((n, n), np.float64)
    for i in range(n):
        for k in range(1, W + 1):
            m[i, (i + k) % n] += OFF[k]
            m[i, (i - k) % n] += OFF[k]
    return m


def plane_weights():
    m = np.zeros((PLANES, 3 * PLANES), np.float64)
    for i in range(PLANES):
        for j in range(3 * PLANES):
            k = abs(i + PLANES - j)
            if 1 <= k <= W:
                m[i, j] = OFF[k]
    m = np.kron(m, np.eye(CY))
    m[:, ROWS : 2 * ROWS] += np.kron(np.eye(PLANES), circulant(CY))
    return m


def halves(m):
    high = m.astype(ml_dtypes.bfloat16)
    low = (m - high.astype(np.float64)).astype(ml_dtypes.bfloat16)
    return high, low


Z_HIGH, Z_LOW = halves(circulant(CZ))
Y_HIGH, Y_LOW = halves(np.kron(np.eye(PLANES), circulant(CY)))
Z3 = np.block([[Z_HIGH, Z_LOW], [Z_HIGH, np.zeros_like(Z_LOW)]])
Y3 = np.concatenate([Y_HIGH, Y_HIGH, Y_LOW], 1)
XY2 = np.concatenate(halves(plane_weights()), 1)
LEFT = np.concatenate([Y3, XY2], 1)


def dot(a, b):
    return jnp.dot(a, b, preferred_element_type=F32)


def along_x(planes, n):
    out = []
    for x in range(W, W + n):
        total = OFF[1] * (planes[x + 1] + planes[x - 1])
        for k in range(2, W + 1):
            total = total + OFF[k] * (planes[x + k] + planes[x - k])
        out.append(total)
    return out


def along_yz(planes, z3, y3):
    n = len(planes)
    field = jnp.concatenate([p[None] for p in planes], 0).reshape(n * CY, CZ)
    high = field.astype(BF16)
    low = (field - high.astype(F32)).astype(BF16)
    z = dot(jnp.concatenate([high, low], 1), z3)
    z = z[:, :CZ] + z[:, CZ:]
    out = []
    for g in range(0, n * CY, ROWS):
        h, l = high[g : g + ROWS], low[g : g + ROWS]
        y = dot(y3, jnp.concatenate([h, l, h], 0)) + z[g : g + ROWS]
        out += [y[i * CY : (i + 1) * CY] for i in range(PLANES)]
    return out


def filter_kernel(
    even, odd, even2, odd2, even3, odd3, s, pot, z3_ref, left_ref, out
):
    count = s.shape[0]
    place = lax.axis_index("y")
    first_of_pair = place % 2 == 0
    first_of_two = place < 2
    z3, left = z3_ref[...], left_ref[...]
    y3, xy2 = left[:, : 3 * ROWS], left[:, 3 * ROWS :]

    def sides(i, one, other, flag):
        before, after = [], []
        for x in range(PLANES):
            a, b = one[i, x].astype(F32), other[i, x].astype(F32)
            before.append(jnp.where(flag, b, a))
            after.append(jnp.where(flag, a, b))
        return before, after

    b1, a1 = sides(count, even, odd, first_of_pair)
    b2, a2 = sides(count, even2, odd2, first_of_two)
    raw = b2 + b1 + [pot[x] for x in range(PLANES)] + a1 + a2
    diag = [(DIAG - SHIFT) + v * (1.0 / HALF) for v in raw]

    def turn(planes, weights):
        inner = planes[W:-W]
        x = along_x(planes, len(inner))
        yz = along_yz(inner, z3, y3)
        return [a + b + d * v for a, b, d, v in zip(x, yz, weights, inner)]

    for i in range(count):
        b1, a1 = sides(i, even, odd, first_of_pair)
        b2, a2 = sides(i, even2, odd2, first_of_two)
        b3, a3 = sides(i, even3, odd3, first_of_pair)
        field = b3 + b2 + b1 + [s[i, x] for x in range(PLANES)] + a1 + a2 + a3
        first = turn(field, diag)
        second = turn(first, diag[W:-W])
        rounded = [
            (2.0 * t - v).astype(BF16) for t, v in zip(second, field[2 * W : -2 * W])
        ]
        blocks = [jnp.concatenate(rounded[k * W : (k + 1) * W], 0) for k in range(3)]
        own = blocks[1]
        xy = dot(xy2, jnp.concatenate(blocks + blocks, 0))
        z = dot(own, z3[:CZ])
        z = z[:, :CZ] + z[:, CZ:]
        for x in range(PLANES):
            rows = slice(x * CY, (x + 1) * CY)
            total = xy[rows] + z[rows] + (diag[2 * W + x] + SHIFT) * rounded[W + x].astype(F32)
            out[i, x] = rounded[W + x]
            out[count + i, x] = total.astype(BF16)


def exchange(array, axes, size, partner):
    return lax.ppermute(array, axes, [(i, partner(i) % size) for i in range(size)])


def even_pairs(array):
    return exchange(array, DOMAIN, 32, lambda d: d ^ 1)


def odd_pairs(array):
    return exchange(array, DOMAIN, 32, lambda d: d + 1 if d % 2 else d - 1)


def even_twos(array):
    return exchange(array, DOMAIN, 32, lambda d: d ^ 2)


def odd_twos(array):
    return exchange(array, DOMAIN, 32, lambda d: d + 2 if d % 4 >= 2 else d - 2)


def even_threes(array):
    return exchange(array, DOMAIN, 32, lambda d: d - 3 if d % 2 else d + 3)


def odd_threes(array):
    return exchange(array, DOMAIN, 32, lambda d: d + 3 if d % 2 else d - 3)


def vmem(n=1):
    return [pl.BlockSpec(memory_space=pltpu.VMEM)] * n


def filter_own(pairs, twos, threes, s, pot):
    constants = [jnp.asarray(m) for m in (Z3, LEFT)]
    return pl.pallas_call(
        filter_kernel,
        out_shape=jax.ShapeDtypeStruct((2 * s.shape[0], *s.shape[1:]), BF16),
        in_specs=vmem(10),
        out_specs=vmem()[0],
        compiler_params=pltpu.CompilerParams(vmem_limit_bytes=16 << 20),
        cost_estimate=pl.CostEstimate(flops=400_000_000, bytes_accessed=1_500_000, transcendentals=0),
        name="filter_own",
    )(*pairs, *twos, *threes, s, pot, *constants)


def body(states, potential, slab):
    count = states.shape[0]
    low = states.astype(BF16)
    near = jnp.concatenate([low, potential.astype(BF16)[None]], axis=0)
    pairs = even_pairs(near), odd_pairs(near)
    twos = even_twos(near), odd_twos(near)
    threes = even_threes(low), odd_threes(low)
    both = filter_own(pairs, twos, threes, states, potential)
    mine = lax.all_gather(both, "z_hi", axis=0, tiled=True)
    theirs = lax.optimization_barrier(exchange(mine, "core", 2, lambda i: i ^ 1))

    n = slab.shape[0]

    def products(block):
        return lax.dot_general(
            block.reshape(block.shape[0], -1),
            slab.reshape(n, -1),
            (((1,), (1,)), ((), ())),
            preferred_element_type=F32,
        )

    out = lax.optimization_barrier((products(mine), products(theirs)))
    pair = jnp.stack(out).reshape(2, 4, 2, count, n) * (1.0 / np.sqrt(np.float32(CELLS)))
    pair = jnp.where(lax.axis_index("core") == 1, jnp.flip(pair, 0), pair)
    term = jnp.transpose(pair, (1, 0, 3, 2, 4)).reshape(32, 2 * n)
    parts = lax.all_to_all(term, DOMAIN, 0, 0, tiled=True)
    share = jnp.sum(parts, axis=0, keepdims=True)
    return share[:, :n], share[:, n:]


def solution(mesh):
    fine = Mesh(mesh.devices.reshape(4, 2, 2, 4, 4), ("z_hi", "core", "z_lo", "x", "y"))
    placed = (P(BAND, DOMAIN, None, None), P(DOMAIN, None, None), P(BAND, DOMAIN, None, None))
    return jax.shard_map(
        body,
        mesh=fine,
        in_specs=placed,
        out_specs=(P(DOMAIN, BAND), P(DOMAIN, BAND)),
        check_vma=False,
    )
```

```python
import jax
import jax.numpy as jnp
import ml_dtypes
import numpy as np
from jax import lax
from jax.experimental import pallas as pl
from jax.experimental.pallas import tpu as pltpu
from jax.sharding import Mesh, PartitionSpec as P

COEFS = (
    -5369.0 / 1800.0,
    12.0 / 7.0,
    -15.0 / 56.0,
    10.0 / 189.0,
    -1.0 / 112.0,
    2.0 / 1925.0,
    -1.0 / 16632.0,
)
SPACING = 0.5
CENTER = 27.5
HALF = 22.5
KIN = -0.5 / SPACING**2
OFF = tuple(KIN * c / HALF for c in COEFS)
DIAG = 3.0 * KIN * COEFS[0] / HALF
SHIFT = CENTER / HALF
BAND = ("z_hi", "core")
DOMAIN = ("z_lo", "x", "y")
CELLS = 393216
W = 6
CY, CZ, PLANES = 16, 128, 6
ROWS = PLANES * CY
BF16, F32 = jnp.bfloat16, jnp.float32


def circulant(n):
    m = np.zeros((n, n), np.float64)
    for i in range(n):
        for k in range(1, W + 1):
            m[i, (i + k) % n] += OFF[k]
            m[i, (i - k) % n] += OFF[k]
    return m


def plane_weights():
    m = np.zeros((PLANES, 3 * PLANES), np.float64)
    for i in range(PLANES):
        for j in range(3 * PLANES):
            k = abs(i + PLANES - j)
            if 1 <= k <= W:
                m[i, j] = OFF[k]
    m = np.kron(m, np.eye(CY))
    m[:, ROWS : 2 * ROWS] += np.kron(np.eye(PLANES), circulant(CY))
    return m


def halves(m):
    high = m.astype(ml_dtypes.bfloat16)
    low = (m - high.astype(np.float64)).astype(ml_dtypes.bfloat16)
    return high, low


Z_HIGH, Z_LOW = halves(circulant(CZ))
Y_HIGH, Y_LOW = halves(np.kron(np.eye(PLANES), circulant(CY)))
Z3 = np.block([[Z_HIGH, Z_LOW], [Z_HIGH, np.zeros_like(Z_LOW)]])
Y3 = np.concatenate([Y_HIGH, Y_HIGH, Y_LOW], 1)
XY2 = np.concatenate(halves(plane_weights()), 1)
LEFT = np.concatenate([Y3, XY2], 1)


def dot(a, b):
    return jnp.dot(a, b, preferred_element_type=F32)


def along_x(planes, n):
    out = []
    for x in range(W, W + n):
        total = OFF[1] * (planes[x + 1] + planes[x - 1])
        for k in range(2, W + 1):
            total = total + OFF[k] * (planes[x + k] + planes[x - k])
        out.append(total)
    return out


def along_yz(pair, z3, left, exact):
    out = [[] for _ in pair]
    for block in range(len(pair[0]) // PLANES):
        part = slice(block * PLANES, (block + 1) * PLANES)
        fields = [jnp.concatenate(planes[part], 0) for planes in pair]
        high = [f.astype(BF16) for f in fields]
        wide = jnp.concatenate(high, 1)
        if exact(block):
            y = dot(left[:, ROWS : 3 * ROWS], jnp.concatenate([wide, wide], 0))
            z = dot(jnp.concatenate(high, 0), z3[:CZ])
        else:
            low = [(f - h.astype(F32)).astype(BF16) for f, h in zip(fields, high)]
            rest = jnp.concatenate(low, 1)
            y = dot(left[:, : 3 * ROWS], jnp.concatenate([wide, rest, wide], 0))
            z = dot(jnp.concatenate([jnp.concatenate(high, 0), jnp.concatenate(low, 0)], 1), z3)
        z = z[:, :CZ] + z[:, CZ:]
        for k in range(len(pair)):
            total = y[:, k * CZ : (k + 1) * CZ] + z[k * ROWS : (k + 1) * ROWS]
            out[k].extend(total[i * CY : (i + 1) * CY] for i in range(PLANES))
    return out


def filter_kernel(
    even, odd, even2, odd2, even3, odd3, s, pot, z3_ref, left_ref, out
):
    count = s.shape[0]
    place = lax.axis_index("y")
    first_of_pair = place % 2 == 0
    first_of_two = place < 2
    z3, left = z3_ref[...], left_ref[...]
    xy2 = left[:, 3 * ROWS :]

    def sides(i, one, other, flag):
        before, after = [], []
        for x in range(PLANES):
            a, b = one[i, x].astype(F32), other[i, x].astype(F32)
            before.append(jnp.where(flag, b, a))
            after.append(jnp.where(flag, a, b))
        return before, after

    b1, a1 = sides(count, even, odd, first_of_pair)
    b2, a2 = sides(count, even2, odd2, first_of_two)
    raw = b2 + b1 + [pot[x] for x in range(PLANES)] + a1 + a2
    diag = [(DIAG - SHIFT) + v * (1.0 / HALF) for v in raw]

    def turn(pair, weights, exact):
        inner = [planes[W:-W] for planes in pair]
        yz = along_yz(inner, z3, left, exact)
        return [
            [a + b + d * v for a, b, d, v in zip(along_x(p, len(v_in)), b_in, weights, v_in)]
            for p, v_in, b_in in zip(pair, inner, yz)
        ]

    for i in range(0, count, 4):
        pair = []
        for j in range(i, i + 4):
            b1, a1 = sides(j, even, odd, first_of_pair)
            b2, a2 = sides(j, even2, odd2, first_of_two)
            b3, a3 = sides(j, even3, odd3, first_of_pair)
            pair.append(b3 + b2 + b1 + [s[j, x] for x in range(PLANES)] + a1 + a2 + a3)
        first = turn(pair, diag, lambda block: block != 2)
        second = turn(first, diag[W:-W], lambda block: False)
        rounded = [
            [(2.0 * t - v).astype(BF16) for t, v in zip(turned, field[2 * W : -2 * W])]
            for turned, field in zip(second, pair)
        ]
        blocks = [[jnp.concatenate(r[k * W : (k + 1) * W], 0) for k in range(3)] for r in rounded]
        wide = [jnp.concatenate([b[k] for b in blocks], 1) for k in range(3)]
        xy = dot(xy2, jnp.concatenate(wide + wide, 0))
        z = dot(jnp.concatenate([b[1] for b in blocks], 0), z3[:CZ])
        z = z[:, :CZ] + z[:, CZ:]
        for j in range(4):
            for x in range(PLANES):
                rows = slice(x * CY, (x + 1) * CY)
                total = xy[rows, j * CZ : (j + 1) * CZ] + z[j * ROWS + x * CY : j * ROWS + (x + 1) * CY]
                own = rounded[j][W + x]
                total = total + (diag[2 * W + x] + SHIFT) * own.astype(F32)
                out[i + j, x] = own
                out[count + i + j, x] = total.astype(BF16)


def exchange(array, axes, size, partner):
    return lax.ppermute(array, axes, [(i, partner(i) % size) for i in range(size)])


def even_pairs(array):
    return exchange(array, DOMAIN, 32, lambda d: d ^ 1)


def odd_pairs(array):
    return exchange(array, DOMAIN, 32, lambda d: d + 1 if d % 2 else d - 1)


def even_twos(array):
    return exchange(array, DOMAIN, 32, lambda d: d ^ 2)


def odd_twos(array):
    return exchange(array, DOMAIN, 32, lambda d: d + 2 if d % 4 >= 2 else d - 2)


def even_threes(array):
    return exchange(array, DOMAIN, 32, lambda d: d - 3 if d % 2 else d + 3)


def odd_threes(array):
    return exchange(array, DOMAIN, 32, lambda d: d + 3 if d % 2 else d - 3)


def vmem(n=1):
    return [pl.BlockSpec(memory_space=pltpu.VMEM)] * n


def filter_own(pairs, twos, threes, s, pot):
    constants = [jnp.asarray(m) for m in (Z3, LEFT)]
    return pl.pallas_call(
        filter_kernel,
        out_shape=jax.ShapeDtypeStruct((2 * s.shape[0], *s.shape[1:]), BF16),
        in_specs=vmem(10),
        out_specs=vmem()[0],
        compiler_params=pltpu.CompilerParams(vmem_limit_bytes=16 << 20),
        cost_estimate=pl.CostEstimate(flops=400_000_000, bytes_accessed=1_500_000, transcendentals=0),
        name="filter_own",
    )(*pairs, *twos, *threes, s, pot, *constants)


def body(states, potential, slab):
    count = states.shape[0]
    low = states.astype(BF16)
    near = jnp.concatenate([low, potential.astype(BF16)[None]], axis=0)
    pairs = even_pairs(near), odd_pairs(near)
    twos = even_twos(near), odd_twos(near)
    threes = even_threes(low), odd_threes(low)
    both = filter_own(pairs, twos, threes, states, potential)
    mine = lax.all_gather(both, "z_hi", axis=0, tiled=True)
    theirs = lax.optimization_barrier(exchange(mine, "core", 2, lambda i: i ^ 1))

    n = slab.shape[0]

    def products(block):
        return lax.dot_general(
            block.reshape(block.shape[0], -1),
            slab.reshape(n, -1),
            (((1,), (1,)), ((), ())),
            preferred_element_type=F32,
        )

    out = lax.optimization_barrier((products(mine), products(theirs)))
    pair = jnp.stack(out).reshape(2, 4, 2, count, n) * (1.0 / np.sqrt(np.float32(CELLS)))
    pair = jnp.where(lax.axis_index("core") == 1, jnp.flip(pair, 0), pair)
    term = jnp.transpose(pair, (1, 0, 3, 2, 4)).reshape(32, 2 * n)
    parts = lax.all_to_all(term, DOMAIN, 0, 0, tiled=True)
    share = jnp.sum(parts, axis=0, keepdims=True)
    return share[:, :n], share[:, n:]


def solution(mesh):
    fine = Mesh(mesh.devices.reshape(4, 2, 2, 4, 4), ("z_hi", "core", "z_lo", "x", "y"))
    placed = (P(BAND, DOMAIN, None, None), P(DOMAIN, None, None), P(BAND, DOMAIN, None, None))
    return jax.shard_map(
        body,
        mesh=fine,
        in_specs=placed,
        out_specs=(P(DOMAIN, BAND), P(DOMAIN, BAND)),
        check_vma=False,
    )
```

```python
import jax
import jax.numpy as jnp
import ml_dtypes
import numpy as np
from jax import lax
from jax.experimental import pallas as pl
from jax.experimental.pallas import tpu as pltpu
from jax.sharding import Mesh, PartitionSpec as P

COEFS = (
    -5369.0 / 1800.0,
    12.0 / 7.0,
    -15.0 / 56.0,
    10.0 / 189.0,
    -1.0 / 112.0,
    2.0 / 1925.0,
    -1.0 / 16632.0,
)
SPACING = 0.5
CENTER = 27.5
HALF = 22.5
KIN = -0.5 / SPACING**2
OFF = tuple(KIN * c / HALF for c in COEFS)
DIAG = 3.0 * KIN * COEFS[0] / HALF
SHIFT = CENTER / HALF
BAND = ("z_hi", "core")
DOMAIN = ("z_lo", "x", "y")
CELLS = 393216
W = 6
CY, CZ, PLANES = 16, 128, 6
ROWS = PLANES * CY
BF16, F32 = jnp.bfloat16, jnp.float32


def circulant(n):
    m = np.zeros((n, n), np.float64)
    for i in range(n):
        for k in range(1, W + 1):
            m[i, (i + k) % n] += OFF[k]
            m[i, (i - k) % n] += OFF[k]
    return m


def plane_weights():
    m = np.zeros((PLANES, 3 * PLANES), np.float64)
    for i in range(PLANES):
        for j in range(3 * PLANES):
            k = abs(i + PLANES - j)
            if 1 <= k <= W:
                m[i, j] = OFF[k]
    m = np.kron(m, np.eye(CY))
    m[:, ROWS : 2 * ROWS] += np.kron(np.eye(PLANES), circulant(CY))
    return m


def halves(m):
    high = m.astype(ml_dtypes.bfloat16)
    low = (m - high.astype(np.float64)).astype(ml_dtypes.bfloat16)
    return high, low


Z_HIGH, Z_LOW = halves(circulant(CZ))
Y_HIGH, Y_LOW = halves(np.kron(np.eye(PLANES), circulant(CY)))
Z3 = np.block([[Z_HIGH, Z_LOW], [Z_HIGH, np.zeros_like(Z_LOW)]])
Y3 = np.concatenate([Y_HIGH, Y_HIGH, Y_LOW], 1)
XY2 = np.concatenate(halves(plane_weights()), 1)
LEFT = np.concatenate([Y3, XY2], 1)


def dot(a, b):
    return jnp.dot(a, b, preferred_element_type=F32)


def along_x(planes, n):
    out = []
    for x in range(W, W + n):
        total = OFF[1] * (planes[x + 1] + planes[x - 1])
        for k in range(2, W + 1):
            total = total + OFF[k] * (planes[x + k] + planes[x - k])
        out.append(total)
    return out


def along_yz(pair, z3, left, exact):
    out = [[] for _ in pair]
    for block in range(len(pair[0]) // PLANES):
        part = slice(block * PLANES, (block + 1) * PLANES)
        fields = [jnp.concatenate(planes[part], 0) for planes in pair]
        high = [f.astype(BF16) for f in fields]
        wide = jnp.concatenate(high, 1)
        if exact(block):
            y = dot(left[:, ROWS : 3 * ROWS], jnp.concatenate([wide, wide], 0))
            z = dot(jnp.concatenate(high, 0), z3[:CZ])
        else:
            low = [(f - h.astype(F32)).astype(BF16) for f, h in zip(fields, high)]
            rest = jnp.concatenate(low, 1)
            y = dot(left[:, : 3 * ROWS], jnp.concatenate([wide, rest, wide], 0))
            z = dot(jnp.concatenate([jnp.concatenate(high, 0), jnp.concatenate(low, 0)], 1), z3)
        z = z[:, :CZ] + z[:, CZ:]
        for k in range(len(pair)):
            total = y[:, k * CZ : (k + 1) * CZ] + z[k * ROWS : (k + 1) * ROWS]
            out[k].extend(total[i * CY : (i + 1) * CY] for i in range(PLANES))
    return out


def sides(i, one, other, flag):
    before, after = [], []
    for x in range(PLANES):
        a, b = one[i, x].astype(F32), other[i, x].astype(F32)
        before.append(jnp.where(flag, b, a))
        after.append(jnp.where(flag, a, b))
    return before, after


def weights(values):
    return [(DIAG - SHIFT) + v * (1.0 / HALF) for v in values]


def near_kernel(even, odd, s, pot, z3_ref, left_ref, out):
    count = s.shape[0]
    flag = lax.axis_index("y") % 2 == 0
    b1, a1 = sides(count, even, odd, flag)
    diag = weights(b1 + [pot[x] for x in range(PLANES)] + a1)
    fields = []
    for i in range(count):
        b1, a1 = sides(i, even, odd, flag)
        fields.append(b1 + [s[i, x] for x in range(PLANES)] + a1)
    yz = along_yz(fields, z3_ref[...], left_ref[...], lambda block: block != 1)
    for i in range(count):
        x_terms = along_x(fields[i], PLANES)
        for p in range(3 * PLANES):
            total = yz[i][p] + diag[p] * fields[i][p]
            if W <= p < W + PLANES:
                total = total + x_terms[p - W]
            out[i, p] = total


def filter_kernel(
    even, odd, even2, odd2, even3, odd3, s, pot, near, z3_ref, left_ref, out
):
    count = s.shape[0]
    place = lax.axis_index("y")
    first_of_pair = place % 2 == 0
    first_of_two = place < 2
    z3, left = z3_ref[...], left_ref[...]
    xy2 = left[:, 3 * ROWS :]

    b1, a1 = sides(count, even, odd, first_of_pair)
    b2, a2 = sides(count, even2, odd2, first_of_two)
    diag = weights(b2 + b1 + [pot[x] for x in range(PLANES)] + a1 + a2)

    fields, outer = [], []
    for i in range(count):
        b1, a1 = sides(i, even, odd, first_of_pair)
        b2, a2 = sides(i, even2, odd2, first_of_two)
        b3, a3 = sides(i, even3, odd3, first_of_pair)
        fields.append(b3 + b2 + b1 + [s[i, x] for x in range(PLANES)] + a1 + a2 + a3)
        outer.append(b2 + a2)
    yz = along_yz(outer, z3, left, lambda block: True)
    first = []
    for i in range(count):
        planes = []
        for p in range(5 * PLANES):
            block = p // PLANES
            if block in (0, 4):
                k = p if block == 0 else p - 3 * PLANES
                total = yz[i][k] + diag[p] * fields[i][p + W]
            else:
                total = near[i, p - PLANES]
            if block != 2:
                total = total + along_x(fields[i][p : p + 2 * W + 1], 1)[0]
            planes.append(total)
        first.append(planes)
    inner = [planes[W:-W] for planes in first]
    yz = along_yz(inner, z3, left, lambda block: False)
    rounded = []
    for i in range(count):
        x_terms = along_x(first[i], 3 * PLANES)
        turned = [a + b + d * v for a, b, d, v in zip(x_terms, yz[i], diag[W:-W], inner[i])]
        own = fields[i][2 * W : -2 * W]
        rounded.append([(2.0 * t - v).astype(BF16) for t, v in zip(turned, own)])
    blocks = [[jnp.concatenate(r[k * W : (k + 1) * W], 0) for k in range(3)] for r in rounded]
    wide = [jnp.concatenate([b[k] for b in blocks], 1) for k in range(3)]
    xy = dot(xy2, jnp.concatenate(wide + wide, 0))
    z = dot(jnp.concatenate([b[1] for b in blocks], 0), z3[:CZ])
    z = z[:, :CZ] + z[:, CZ:]
    for j in range(count):
        for x in range(PLANES):
            rows = slice(x * CY, (x + 1) * CY)
            total = xy[rows, j * CZ : (j + 1) * CZ] + z[j * ROWS + x * CY : j * ROWS + (x + 1) * CY]
            own = rounded[j][W + x]
            total = total + (diag[2 * W + x] + SHIFT) * own.astype(F32)
            out[j, x] = own
            out[count + j, x] = total.astype(BF16)


def exchange(array, axes, size, partner):
    return lax.ppermute(array, axes, [(i, partner(i) % size) for i in range(size)])


def even_pairs(array):
    return exchange(array, DOMAIN, 32, lambda d: d ^ 1)


def odd_pairs(array):
    return exchange(array, DOMAIN, 32, lambda d: d + 1 if d % 2 else d - 1)


def even_twos(array):
    return exchange(array, DOMAIN, 32, lambda d: d ^ 2)


def odd_twos(array):
    return exchange(array, DOMAIN, 32, lambda d: d + 2 if d % 4 >= 2 else d - 2)


def even_threes(array):
    return exchange(array, DOMAIN, 32, lambda d: d - 3 if d % 2 else d + 3)


def odd_threes(array):
    return exchange(array, DOMAIN, 32, lambda d: d + 3 if d % 2 else d - 3)


def vmem(n=1):
    return [pl.BlockSpec(memory_space=pltpu.VMEM)] * n


def near_terms(pairs, s, pot):
    count, planes, *cells = s.shape
    return pl.pallas_call(
        near_kernel,
        out_shape=jax.ShapeDtypeStruct((count, 3 * planes, *cells), F32),
        in_specs=vmem(6),
        out_specs=vmem()[0],
        compiler_params=pltpu.CompilerParams(vmem_limit_bytes=16 << 20),
        cost_estimate=pl.CostEstimate(flops=4000000000, bytes_accessed=1_500_000, transcendentals=0),
        name="near_terms",
    )(*pairs, s, pot, jnp.asarray(Z3), jnp.asarray(LEFT))


def filter_own(pairs, twos, threes, s, pot, near):
    constants = [jnp.asarray(m) for m in (Z3, LEFT)]
    return pl.pallas_call(
        filter_kernel,
        out_shape=jax.ShapeDtypeStruct((2 * s.shape[0], *s.shape[1:]), BF16),
        in_specs=vmem(11),
        out_specs=vmem()[0],
        compiler_params=pltpu.CompilerParams(vmem_limit_bytes=16 << 20),
        cost_estimate=pl.CostEstimate(flops=5_000_000_000, bytes_accessed=1_500_000, transcendentals=0),
        name="filter_own",
    )(*pairs, *twos, *threes, s, pot, near, *constants)


def body(states, potential, slab):
    count = states.shape[0]
    low = states.astype(BF16)
    near = jnp.concatenate([low, potential.astype(BF16)[None]], axis=0)
    pairs = even_pairs(near), odd_pairs(near)
    twos = even_twos(near), odd_twos(near)
    threes = even_threes(low), odd_threes(low)
    near = near_terms(pairs, states, potential)
    other_slab = lax.optimization_barrier(exchange(slab, "core", 2, lambda i: i ^ 1))
    both = filter_own(pairs, twos, threes, states, potential, near)
    mine = lax.all_gather(both, "z_hi", axis=0, tiled=True)
    n = slab.shape[0]

    def products(block):
        out = lax.dot_general(
            mine.reshape(mine.shape[0], -1),
            block.reshape(n, -1),
            (((1,), (1,)), ((), ())),
            preferred_element_type=F32,
        )
        return lax.optimization_barrier(out)

    out = products(slab), exchange(products(other_slab), "core", 2, lambda i: i ^ 1)
    pair = jnp.stack(out).reshape(2, 4, 2, count, n) * (1.0 / np.sqrt(np.float32(CELLS)))
    pair = jnp.where(lax.axis_index("core") == 1, jnp.flip(pair, 0), pair)
    term = jnp.transpose(pair, (1, 0, 3, 2, 4)).reshape(32, 2 * n)
    parts = lax.all_to_all(term, DOMAIN, 0, 0, tiled=True)
    share = jnp.sum(parts, axis=0, keepdims=True)
    return share[:, :n], share[:, n:]


def solution(mesh):
    fine = Mesh(mesh.devices.reshape(4, 2, 2, 4, 4), ("z_hi", "core", "z_lo", "x", "y"))
    placed = (P(BAND, DOMAIN, None, None), P(DOMAIN, None, None), P(BAND, DOMAIN, None, None))
    return jax.shard_map(
        body,
        mesh=fine,
        in_specs=placed,
        out_specs=(P(DOMAIN, BAND), P(DOMAIN, BAND)),
        check_vma=False,
    )
```

```python
import jax
import jax.numpy as jnp
import ml_dtypes
import numpy as np
from jax import lax
from jax.experimental import pallas as pl
from jax.experimental.pallas import tpu as pltpu
from jax.sharding import Mesh, PartitionSpec as P

COEFS = (
    -5369.0 / 1800.0,
    12.0 / 7.0,
    -15.0 / 56.0,
    10.0 / 189.0,
    -1.0 / 112.0,
    2.0 / 1925.0,
    -1.0 / 16632.0,
)
SPACING = 0.5
CENTER = 27.5
HALF = 22.5
KIN = -0.5 / SPACING**2
OFF = tuple(KIN * c / HALF for c in COEFS)
DIAG = 3.0 * KIN * COEFS[0] / HALF
SHIFT = CENTER / HALF
BAND = ("z_hi", "core")
DOMAIN = ("z_lo", "x", "y")
CELLS = 393216
W = 6
CY, CZ, PLANES = 16, 128, 6
ROWS = PLANES * CY
BF16, F32 = jnp.bfloat16, jnp.float32


def circulant(n):
    m = np.zeros((n, n), np.float64)
    for i in range(n):
        for k in range(1, W + 1):
            m[i, (i + k) % n] += OFF[k]
            m[i, (i - k) % n] += OFF[k]
    return m


def plane_weights():
    m = np.zeros((PLANES, 3 * PLANES), np.float64)
    for i in range(PLANES):
        for j in range(3 * PLANES):
            k = abs(i + PLANES - j)
            if 1 <= k <= W:
                m[i, j] = OFF[k]
    m = np.kron(m, np.eye(CY))
    m[:, ROWS : 2 * ROWS] += np.kron(np.eye(PLANES), circulant(CY))
    return m


def halves(m):
    high = m.astype(ml_dtypes.bfloat16)
    low = (m - high.astype(np.float64)).astype(ml_dtypes.bfloat16)
    return high, low


Z_HIGH, Z_LOW = halves(circulant(CZ))
Y_HIGH, Y_LOW = halves(np.kron(np.eye(PLANES), circulant(CY)))
Z3 = np.block([[Z_HIGH, Z_LOW], [Z_HIGH, np.zeros_like(Z_LOW)]])
Y3 = np.concatenate([Y_HIGH, Y_HIGH, Y_LOW], 1)
XY2 = np.concatenate(halves(plane_weights()), 1)
LEFT = np.concatenate([Y3, XY2], 1)


def dot(a, b):
    return jnp.dot(a, b, preferred_element_type=F32)


def along_x(planes, n):
    out = []
    for x in range(W, W + n):
        total = OFF[1] * (planes[x + 1] + planes[x - 1])
        for k in range(2, W + 1):
            total = total + OFF[k] * (planes[x + k] + planes[x - k])
        out.append(total)
    return out


def along_yz(pair, z3, left, exact):
    out = [[] for _ in pair]
    for block in range(len(pair[0]) // PLANES):
        part = slice(block * PLANES, (block + 1) * PLANES)
        fields = [jnp.concatenate(planes[part], 0) for planes in pair]
        high = [f.astype(BF16) for f in fields]
        wide = jnp.concatenate(high, 1)
        if exact(block):
            y = dot(left[:, ROWS : 3 * ROWS], jnp.concatenate([wide, wide], 0))
            z = dot(jnp.concatenate(high, 0), z3[:CZ])
        else:
            low = [(f - h.astype(F32)).astype(BF16) for f, h in zip(fields, high)]
            rest = jnp.concatenate(low, 1)
            y = dot(left[:, : 3 * ROWS], jnp.concatenate([wide, rest, wide], 0))
            z = dot(jnp.concatenate([jnp.concatenate(high, 0), jnp.concatenate(low, 0)], 1), z3)
        z = z[:, :CZ] + z[:, CZ:]
        for k in range(len(pair)):
            total = y[:, k * CZ : (k + 1) * CZ] + z[k * ROWS : (k + 1) * ROWS]
            out[k].extend(total[i * CY : (i + 1) * CY] for i in range(PLANES))
    return out


def sides(i, one, other, flag):
    before, after = [], []
    for x in range(PLANES):
        a, b = one[i, x].astype(F32), other[i, x].astype(F32)
        before.append(jnp.where(flag, b, a))
        after.append(jnp.where(flag, a, b))
    return before, after


def weights(values):
    return [(DIAG - SHIFT) + v * (1.0 / HALF) for v in values]


def near_kernel(even, odd, s, pot, z3_ref, left_ref, out):
    count = s.shape[0]
    flag = lax.axis_index("y") % 2 == 0
    b1, a1 = sides(count, even, odd, flag)
    diag = weights(b1 + [pot[x] for x in range(PLANES)] + a1)
    fields = []
    for i in range(count):
        b1, a1 = sides(i, even, odd, flag)
        fields.append(b1 + [s[i, x] for x in range(PLANES)] + a1)
    yz = along_yz(fields, z3_ref[...], left_ref[...], lambda block: block != 1)
    for i in range(count):
        x_terms = along_x(fields[i], PLANES)
        for p in range(3 * PLANES):
            total = yz[i][p] + diag[p] * fields[i][p]
            if W <= p < W + PLANES:
                total = total + x_terms[p - W]
            out[i, p] = total


def filter_kernel(
    even, odd, even2, odd2, even3, odd3, s, pot, near, z3_ref, left_ref, out
):
    count = s.shape[0]
    place = lax.axis_index("y")
    first_of_pair = place % 2 == 0
    first_of_two = place < 2
    z3, left = z3_ref[...], left_ref[...]
    xy2 = left[:, 3 * ROWS :]

    b1, a1 = sides(count, even, odd, first_of_pair)
    b2, a2 = sides(count, even2, odd2, first_of_two)
    diag = weights(b2 + b1 + [pot[x] for x in range(PLANES)] + a1 + a2)

    fields, outer = [], []
    for i in range(count):
        b1, a1 = sides(i, even, odd, first_of_pair)
        b2, a2 = sides(i, even2, odd2, first_of_two)
        b3, a3 = sides(i, even3, odd3, first_of_pair)
        fields.append(b3 + b2 + b1 + [s[i, x] for x in range(PLANES)] + a1 + a2 + a3)
        outer.append(b2 + a2)
    yz = along_yz(outer, z3, left, lambda block: True)
    first = []
    for i in range(count):
        planes = []
        for p in range(5 * PLANES):
            block = p // PLANES
            if block in (0, 4):
                k = p if block == 0 else p - 3 * PLANES
                total = yz[i][k] + diag[p] * fields[i][p + W]
            else:
                total = near[i, p - PLANES]
            if block != 2:
                total = total + along_x(fields[i][p : p + 2 * W + 1], 1)[0]
            planes.append(total)
        first.append(planes)
    inner = [planes[W:-W] for planes in first]
    yz = along_yz(inner, z3, left, lambda block: False)
    rounded = []
    for i in range(count):
        x_terms = along_x(first[i], 3 * PLANES)
        turned = [a + b + d * v for a, b, d, v in zip(x_terms, yz[i], diag[W:-W], inner[i])]
        own = fields[i][2 * W : -2 * W]
        rounded.append([(2.0 * t - v).astype(BF16) for t, v in zip(turned, own)])
    blocks = [[jnp.concatenate(r[k * W : (k + 1) * W], 0) for k in range(3)] for r in rounded]
    wide = [jnp.concatenate([b[k] for b in blocks], 1) for k in range(3)]
    xy = dot(xy2, jnp.concatenate(wide + wide, 0))
    z = dot(jnp.concatenate([b[1] for b in blocks], 0), z3[:CZ])
    z = z[:, :CZ] + z[:, CZ:]
    for j in range(count):
        for x in range(PLANES):
            rows = slice(x * CY, (x + 1) * CY)
            total = xy[rows, j * CZ : (j + 1) * CZ] + z[j * ROWS + x * CY : j * ROWS + (x + 1) * CY]
            own = rounded[j][W + x]
            total = total + (diag[2 * W + x] + SHIFT) * own.astype(F32)
            out[j, x] = own
            out[count + j, x] = total.astype(BF16)


def exchange(array, axes, size, partner):
    return lax.ppermute(array, axes, [(i, partner(i) % size) for i in range(size)])


def even_pairs(array):
    return exchange(array, DOMAIN, 32, lambda d: d ^ 1)


def odd_pairs(array):
    return exchange(array, DOMAIN, 32, lambda d: d + 1 if d % 2 else d - 1)


def even_twos(array):
    return exchange(array, DOMAIN, 32, lambda d: d ^ 2)


def odd_twos(array):
    return exchange(array, DOMAIN, 32, lambda d: d + 2 if d % 4 >= 2 else d - 2)


def even_threes(array):
    return exchange(array, DOMAIN, 32, lambda d: d - 3 if d % 2 else d + 3)


def odd_threes(array):
    return exchange(array, DOMAIN, 32, lambda d: d + 3 if d % 2 else d - 3)


def vmem(n=1):
    return [pl.BlockSpec(memory_space=pltpu.VMEM)] * n


def near_terms(pairs, s, pot):
    count, planes, *cells = s.shape
    return pl.pallas_call(
        near_kernel,
        out_shape=jax.ShapeDtypeStruct((count, 3 * planes, *cells), F32),
        in_specs=vmem(6),
        out_specs=vmem()[0],
        compiler_params=pltpu.CompilerParams(vmem_limit_bytes=16 << 20),
        cost_estimate=pl.CostEstimate(flops=4000000000, bytes_accessed=1_500_000, transcendentals=0),
        name="near_terms",
    )(*pairs, s, pot, jnp.asarray(Z3), jnp.asarray(LEFT))


def filter_own(pairs, twos, threes, s, pot, near):
    constants = [jnp.asarray(m) for m in (Z3, LEFT)]
    return pl.pallas_call(
        filter_kernel,
        out_shape=jax.ShapeDtypeStruct((2 * s.shape[0], *s.shape[1:]), BF16),
        in_specs=vmem(11),
        out_specs=vmem()[0],
        compiler_params=pltpu.CompilerParams(vmem_limit_bytes=16 << 20),
        cost_estimate=pl.CostEstimate(flops=5_000_000_000, bytes_accessed=1_500_000, transcendentals=0),
        name="filter_own",
    )(*pairs, *twos, *threes, s, pot, near, *constants)


def body(states, potential, slab):
    count = states.shape[0]
    low = states.astype(BF16)
    near = jnp.concatenate([low, potential.astype(BF16)[None]], axis=0)
    pairs = even_pairs(near), odd_pairs(near)
    twos = even_twos(near), odd_twos(near)
    threes = even_threes(low), odd_threes(low)
    near = near_terms(pairs, states, potential)
    other_slab = exchange(slab, "core", 2, lambda i: i ^ 1)
    slabs = jnp.concatenate([slab, other_slab], axis=0)
    both = filter_own(pairs, twos, threes, states, potential, near)
    mine = lax.all_gather(both, "z_hi", axis=0, tiled=True)
    n = slab.shape[0]

    out = lax.dot_general(
        mine.reshape(mine.shape[0], -1),
        slabs.reshape(2 * n, -1),
        (((1,), (1,)), ((), ())),
        preferred_element_type=F32,
    )
    out = lax.optimization_barrier(out)
    out = out[:, :n], exchange(out[:, n:], "core", 2, lambda i: i ^ 1)
    pair = jnp.stack(out).reshape(2, 4, 2, count, n) * (1.0 / np.sqrt(np.float32(CELLS)))
    pair = jnp.where(lax.axis_index("core") == 1, jnp.flip(pair, 0), pair)
    term = jnp.transpose(pair, (1, 0, 3, 2, 4)).reshape(32, 2 * n)
    parts = lax.all_to_all(term, DOMAIN, 0, 0, tiled=True)
    share = jnp.sum(parts, axis=0, keepdims=True)
    return share[:, :n], share[:, n:]


def solution(mesh):
    fine = Mesh(mesh.devices.reshape(4, 2, 2, 4, 4), ("z_hi", "core", "z_lo", "x", "y"))
    placed = (P(BAND, DOMAIN, None, None), P(DOMAIN, None, None), P(BAND, DOMAIN, None, None))
    return jax.shard_map(
        body,
        mesh=fine,
        in_specs=placed,
        out_specs=(P(DOMAIN, BAND), P(DOMAIN, BAND)),
        check_vma=False,
    )
```

```python
import jax
import jax.numpy as jnp
import ml_dtypes
import numpy as np
from jax import lax
from jax.experimental import pallas as pl
from jax.experimental.pallas import tpu as pltpu
from jax.sharding import Mesh, PartitionSpec as P

COEFS = (
    -5369.0 / 1800.0,
    12.0 / 7.0,
    -15.0 / 56.0,
    10.0 / 189.0,
    -1.0 / 112.0,
    2.0 / 1925.0,
    -1.0 / 16632.0,
)
SPACING = 0.5
CENTER = 27.5
HALF = 22.5
KIN = -0.5 / SPACING**2
OFF = tuple(KIN * c / HALF for c in COEFS)
DIAG = 3.0 * KIN * COEFS[0] / HALF
SHIFT = CENTER / HALF
BAND = ("z_hi", "core")
DOMAIN = ("z_lo", "x", "y")
CELLS = 393216
W = 6
CY, CZ, PLANES = 16, 128, 6
ROWS = PLANES * CY
BF16, F32 = jnp.bfloat16, jnp.float32


def circulant(n):
    m = np.zeros((n, n), np.float64)
    for i in range(n):
        for k in range(1, W + 1):
            m[i, (i + k) % n] += OFF[k]
            m[i, (i - k) % n] += OFF[k]
    return m


def plane_weights():
    m = np.zeros((PLANES, 3 * PLANES), np.float64)
    for i in range(PLANES):
        for j in range(3 * PLANES):
            k = abs(i + PLANES - j)
            if 1 <= k <= W:
                m[i, j] = OFF[k]
    m = np.kron(m, np.eye(CY))
    m[:, ROWS : 2 * ROWS] += np.kron(np.eye(PLANES), circulant(CY))
    return m


def halves(m):
    high = m.astype(ml_dtypes.bfloat16)
    low = (m - high.astype(np.float64)).astype(ml_dtypes.bfloat16)
    return high, low


Z_HIGH, Z_LOW = halves(circulant(CZ))
Y_HIGH, Y_LOW = halves(np.kron(np.eye(PLANES), circulant(CY)))
Z3 = np.block([[Z_HIGH, Z_LOW], [Z_HIGH, np.zeros_like(Z_LOW)]])
Y3 = np.concatenate([Y_HIGH, Y_HIGH, Y_LOW], 1)
XY2 = np.concatenate(halves(plane_weights()), 1)
LEFT = np.concatenate([Y3, XY2], 1)


def dot(a, b):
    return jnp.dot(a, b, preferred_element_type=F32)


def along_x(planes, n):
    out = []
    for x in range(W, W + n):
        total = OFF[1] * (planes[x + 1] + planes[x - 1])
        for k in range(2, W + 1):
            total = total + OFF[k] * (planes[x + k] + planes[x - k])
        out.append(total)
    return out


def along_yz(pair, z3, left, exact):
    out = [[] for _ in pair]
    for block in range(len(pair[0]) // PLANES):
        part = slice(block * PLANES, (block + 1) * PLANES)
        fields = [jnp.concatenate(planes[part], 0) for planes in pair]
        high = [f.astype(BF16) for f in fields]
        wide = jnp.concatenate(high, 1)
        if exact(block):
            y = dot(left[:, ROWS : 3 * ROWS], jnp.concatenate([wide, wide], 0))
            z = dot(jnp.concatenate(high, 0), z3[:CZ])
        else:
            low = [(f - h.astype(F32)).astype(BF16) for f, h in zip(fields, high)]
            rest = jnp.concatenate(low, 1)
            y = dot(left[:, : 3 * ROWS], jnp.concatenate([wide, rest, wide], 0))
            z = dot(jnp.concatenate([jnp.concatenate(high, 0), jnp.concatenate(low, 0)], 1), z3)
        z = z[:, :CZ] + z[:, CZ:]
        for k in range(len(pair)):
            total = y[:, k * CZ : (k + 1) * CZ] + z[k * ROWS : (k + 1) * ROWS]
            out[k].extend(total[i * CY : (i + 1) * CY] for i in range(PLANES))
    return out


def sides(i, one, other, flag):
    before, after = [], []
    for x in range(PLANES):
        a, b = one[i, x].astype(F32), other[i, x].astype(F32)
        before.append(jnp.where(flag, b, a))
        after.append(jnp.where(flag, a, b))
    return before, after


def weights(values):
    return [(DIAG - SHIFT) + v * (1.0 / HALF) for v in values]


def near_kernel(even, odd, s, pot, z3_ref, left_ref, out):
    count = s.shape[0]
    flag = lax.axis_index("y") % 2 == 0
    b1, a1 = sides(count, even, odd, flag)
    diag = weights(b1 + [pot[x] for x in range(PLANES)] + a1)
    fields = []
    for i in range(count):
        b1, a1 = sides(i, even, odd, flag)
        fields.append(b1 + [s[i, x] for x in range(PLANES)] + a1)
    yz = along_yz(fields, z3_ref[...], left_ref[...], lambda block: block != 1)
    for i in range(count):
        x_terms = along_x(fields[i], PLANES)
        for p in range(3 * PLANES):
            total = yz[i][p] + diag[p] * fields[i][p]
            if W <= p < W + PLANES:
                total = total + x_terms[p - W]
            out[i, p] = total


def filter_kernel(
    even, odd, even2, odd2, even3, odd3, s, pot, near, z3_ref, left_ref, out
):
    count = s.shape[0]
    place = lax.axis_index("y")
    first_of_pair = place % 2 == 0
    first_of_two = place < 2
    z3, left = z3_ref[...], left_ref[...]
    xy2 = left[:, 3 * ROWS :]

    b1, a1 = sides(count, even, odd, first_of_pair)
    b2, a2 = sides(count, even2, odd2, first_of_two)
    diag = weights(b2 + b1 + [pot[x] for x in range(PLANES)] + a1 + a2)

    fields, outer = [], []
    for i in range(count):
        b1, a1 = sides(i, even, odd, first_of_pair)
        b2, a2 = sides(i, even2, odd2, first_of_two)
        b3, a3 = sides(i, even3, odd3, first_of_pair)
        fields.append(b3 + b2 + b1 + [s[i, x] for x in range(PLANES)] + a1 + a2 + a3)
        outer.append(b2 + a2)
    yz = along_yz(outer, z3, left, lambda block: True)
    first = []
    for i in range(count):
        planes = []
        for p in range(5 * PLANES):
            block = p // PLANES
            if block in (0, 4):
                k = p if block == 0 else p - 3 * PLANES
                total = yz[i][k] + diag[p] * fields[i][p + W]
            else:
                total = near[i, p - PLANES]
            if block != 2:
                total = total + along_x(fields[i][p : p + 2 * W + 1], 1)[0]
            planes.append(total)
        first.append(planes)
    inner = [planes[W:-W] for planes in first]
    yz = along_yz(inner, z3, left, lambda block: block != 1)
    rounded = []
    for i in range(count):
        x_terms = along_x(first[i], 3 * PLANES)
        turned = [a + b + d * v for a, b, d, v in zip(x_terms, yz[i], diag[W:-W], inner[i])]
        own = fields[i][2 * W : -2 * W]
        rounded.append([(2.0 * t - v).astype(BF16) for t, v in zip(turned, own)])
    blocks = [[jnp.concatenate(r[k * W : (k + 1) * W], 0) for k in range(3)] for r in rounded]
    wide = [jnp.concatenate([b[k] for b in blocks], 1) for k in range(3)]
    xy = dot(xy2, jnp.concatenate(wide + wide, 0))
    z = dot(jnp.concatenate([b[1] for b in blocks], 0), z3[:CZ])
    z = z[:, :CZ] + z[:, CZ:]
    for j in range(count):
        for x in range(PLANES):
            rows = slice(x * CY, (x + 1) * CY)
            total = xy[rows, j * CZ : (j + 1) * CZ] + z[j * ROWS + x * CY : j * ROWS + (x + 1) * CY]
            own = rounded[j][W + x]
            total = total + (diag[2 * W + x] + SHIFT) * own.astype(F32)
            out[j, x] = own
            out[count + j, x] = total.astype(BF16)


def exchange(array, axes, size, partner):
    return lax.ppermute(array, axes, [(i, partner(i) % size) for i in range(size)])


def even_pairs(array):
    return exchange(array, DOMAIN, 32, lambda d: d ^ 1)


def odd_pairs(array):
    return exchange(array, DOMAIN, 32, lambda d: d + 1 if d % 2 else d - 1)


def even_twos(array):
    return exchange(array, DOMAIN, 32, lambda d: d ^ 2)


def odd_twos(array):
    return exchange(array, DOMAIN, 32, lambda d: d + 2 if d % 4 >= 2 else d - 2)


def even_threes(array):
    return exchange(array, DOMAIN, 32, lambda d: d - 3 if d % 2 else d + 3)


def odd_threes(array):
    return exchange(array, DOMAIN, 32, lambda d: d + 3 if d % 2 else d - 3)


def vmem(n=1):
    return [pl.BlockSpec(memory_space=pltpu.VMEM)] * n


def near_terms(pairs, s, pot):
    count, planes, *cells = s.shape
    return pl.pallas_call(
        near_kernel,
        out_shape=jax.ShapeDtypeStruct((count, 3 * planes, *cells), F32),
        in_specs=vmem(6),
        out_specs=vmem()[0],
        compiler_params=pltpu.CompilerParams(vmem_limit_bytes=16 << 20),
        cost_estimate=pl.CostEstimate(flops=4000000000, bytes_accessed=1_500_000, transcendentals=0),
        name="near_terms",
    )(*pairs, s, pot, jnp.asarray(Z3), jnp.asarray(LEFT))


def filter_own(pairs, twos, threes, s, pot, near):
    constants = [jnp.asarray(m) for m in (Z3, LEFT)]
    return pl.pallas_call(
        filter_kernel,
        out_shape=jax.ShapeDtypeStruct((2 * s.shape[0], *s.shape[1:]), BF16),
        in_specs=vmem(11),
        out_specs=vmem()[0],
        compiler_params=pltpu.CompilerParams(vmem_limit_bytes=16 << 20),
        cost_estimate=pl.CostEstimate(flops=5_000_000_000, bytes_accessed=1_500_000, transcendentals=0),
        name="filter_own",
    )(*pairs, *twos, *threes, s, pot, near, *constants)


def body(states, potential, slab):
    count = states.shape[0]
    low = states.astype(BF16)
    near = jnp.concatenate([low, potential.astype(BF16)[None]], axis=0)
    pairs = even_pairs(near), odd_pairs(near)
    twos = even_twos(near), odd_twos(near)
    threes = even_threes(low), odd_threes(low)
    near = near_terms(pairs, states, potential)
    other_slab = lax.optimization_barrier(exchange(slab, "core", 2, lambda i: i ^ 1))
    both = filter_own(pairs, twos, threes, states, potential, near)
    mine = lax.all_gather(both, "z_hi", axis=0, tiled=True)
    n = slab.shape[0]

    def products(block):
        out = lax.dot_general(
            mine.reshape(mine.shape[0], -1),
            block.reshape(n, -1),
            (((1,), (1,)), ((), ())),
            preferred_element_type=F32,
        )
        return lax.optimization_barrier(out)

    out = products(slab), exchange(products(other_slab), "core", 2, lambda i: i ^ 1)
    pair = jnp.stack(out).reshape(2, 4, 2, count, n) * (1.0 / np.sqrt(np.float32(CELLS)))
    pair = jnp.where(lax.axis_index("core") == 1, jnp.flip(pair, 0), pair)
    term = jnp.transpose(pair, (1, 0, 3, 2, 4)).reshape(32, 2 * n)
    parts = lax.all_to_all(term, DOMAIN, 0, 0, tiled=True)
    share = jnp.sum(parts, axis=0, keepdims=True)
    return share[:, :n], share[:, n:]


def solution(mesh):
    fine = Mesh(mesh.devices.reshape(4, 2, 2, 4, 4), ("z_hi", "core", "z_lo", "x", "y"))
    placed = (P(BAND, DOMAIN, None, None), P(DOMAIN, None, None), P(BAND, DOMAIN, None, None))
    return jax.shard_map(
        body,
        mesh=fine,
        in_specs=placed,
        out_specs=(P(DOMAIN, BAND), P(DOMAIN, BAND)),
        check_vma=False,
    )
```
